32 devices in a mesh: group: 8 (over z, y), tensor: 4 (over x, core).
Axes of the slice: x: 2, y: 2, z: 4, core: 2. Of those that a mesh axis runs over, the one named last changes fastest.
Arguments:
- tokens: bfloat16 [16, 128, 4608], P('group', None, 'tensor'), may hold values from -6 to 6
- targets: bfloat16 [16, 128, 4608], P('group', None, 'tensor'), may hold values from -6 to 6
- token_counts: int32 [16], P('group'), may hold values from 1 to 128, as said below
- sample_counts: int32 [16], replicated, may hold values from 1 to 1000
- up_weight: bfloat16 [6912, 4608], P('tensor'), may hold values from -0.09375 to 0.09375
- down_weight: bfloat16 [6912, 4608], P('tensor'), may hold values from -0.078125 to 0.078125
- momentum_up: float32 [6912, 4608], P('tensor', 'group'), may hold values from -6 to 6
- momentum_down: float32 [6912, 4608], P('tensor', 'group'), may hold values from -6 to 6
Outputs:
- new_momentum_up: float32 [6912, 4608], P('tensor', 'group')
- new_momentum_down: float32 [6912, 4608], P('tensor', 'group')
The draws below stay inside these ranges and needn't reach their ends.
Inputs may be any that keep to these rules, and one draw needn't show every extreme that they name: `token_counts`: some client has exactly 128 valid rows and some exactly 1.
All inputs are finite; a program needn't handle non-finite values.
Results may differ from the reference program's by a relative error of at most 0.02.
Values may be sent and summed in bfloat16 or wider, within the bound.
A program may use at most 384 MiB of HBM per device.

```python
import jax
import jax.numpy as jnp
from jax import lax

D = 4608
FFW = 6912
ROWS = 128
CL_GRP = 2
STEPS = 2
CLIENTS = 16
N_GROUP = 8
N_TENSOR = 4


def draw_token_counts(key, part):
    counts = jax.random.randint(key, (CLIENTS,), 1, ROWS + 1, dtype=jnp.int32)
    picked = jax.random.permutation(jax.random.fold_in(key, 7), CLIENTS)
    slots_all = jnp.arange(CLIENTS, dtype=jnp.int32)
    counts = jnp.where(slots_all == picked[0], ROWS, counts)
    counts = jnp.where(slots_all == picked[1], 1, counts)
    return counts.astype(jnp.int32)


def plant(array, own_key, smallest, high):
    longest = array.shape.index(max(array.shape))
    spots = []
    for shift in (0, 1):
        where = [jax.random.randint(jax.random.fold_in(own_key, axis), (), 0, length) for axis, length in enumerate(array.shape)]
        where[longest] = (where[longest] + shift) % array.shape[longest]
        spots.append(tuple(where))
    return array.at[spots[0]].set(smallest).at[spots[1]].set(high)


def shard_levels(own_key, extent, shards, low, largest):
    level, own = 1.0, jax.random.fold_in(own_key, 6)
    for position, shards_of in shards:
        draws = jnp.exp(jax.random.uniform(jax.random.fold_in(own, position), (shards_of,), jnp.float32, low / len(shards), largest / len(shards)))
        level = level * jnp.repeat(draws, extent[position] // shards_of).reshape([-1 if axis == position else 1 for axis in range(len(extent))])
    return level


def normal_values(stream_key, extent, spread, most, cuts=(), held_as=jnp.bfloat16):
    array = jax.random.normal(stream_key, extent, jnp.float32) * spread
    if len(cuts) > 0:
        array = shard_levels(stream_key, extent, cuts, -0.22, 0.18) * array
    return jnp.clip(array, min=-most, max=most).astype(held_as)


def setup_inputs(seed: int = 0) -> dict:
    key_of = jax.random.split(jax.random.key(seed), 9)
    tokens = normal_values(key_of[0], (CLIENTS, ROWS, D), 1.0, 6.0, ((0, 8), (2, 4)))
    targets = normal_values(key_of[1], (CLIENTS, ROWS, D), 1.0, 6.0, ((0, 8), (2, 4)))
    token_counts = draw_token_counts(jax.random.fold_in(key_of[8], 71), 0)
    sample_counts = plant(jax.random.randint(key_of[3], (CLIENTS,), 1, 1001), jax.random.fold_in(key_of[3], 1), 1, 1000).astype(jnp.int32)
    up_weight = normal_values(key_of[4], (FFW, D), D ** -0.5, 0.09375, ((0, 4),))
    down_weight = normal_values(key_of[5], (FFW, D), FFW ** -0.5, 0.078125, ((0, 4),))
    momentum_up = normal_values(key_of[6], (FFW, D), 1.0, 6.0, ((0, 4), (1, 8)), jnp.float32)
    momentum_down = normal_values(key_of[7], (FFW, D), 1.0, 6.0, ((0, 4), (1, 8)), jnp.float32)
    return dict(tokens=tokens, targets=targets, token_counts=token_counts, sample_counts=sample_counts, up_weight=up_weight, down_weight=down_weight, momentum_up=momentum_up, momentum_down=momentum_down)


client_rate = 0.0003
momentum_decay = 0.9


def silu_slope(preact):
    logistic = jax.nn.sigmoid(preact)
    return logistic * (1.0 + preact * (1.0 - logistic))


def client_grads(inputs, target, row_mask, weight_up, weight_down):
    preact = lax.dot_general(inputs, weight_up, (((1,), (1,)), ((), ())), preferred_element_type=jnp.float32)
    hidden = jax.nn.silu(preact).astype(jnp.bfloat16)
    blocks = hidden.astype(jnp.float32).reshape(ROWS, N_TENSOR, FFW // N_TENSOR)
    down_blocks = weight_down.astype(jnp.float32).reshape(N_TENSOR, FFW // N_TENSOR, D)
    pieces = jnp.einsum("rkf,kfd->rkd", blocks, down_blocks, precision=lax.Precision.HIGHEST)
    pieces = lax.optimization_barrier(pieces.astype(jnp.bfloat16)).astype(jnp.float32)
    output = jnp.sum(pieces, axis=1)
    residual = (row_mask * (output - target.astype(jnp.float32))).astype(jnp.bfloat16)
    grad_down = lax.dot_general(hidden, residual, (((0,), (0,)), ((), ())), preferred_element_type=jnp.float32)
    back_grad = lax.dot_general(residual, weight_down, (((1,), (1,)), ((), ())), preferred_element_type=jnp.float32)
    slopes = (back_grad * silu_slope(preact)).astype(jnp.bfloat16)
    grad_up = lax.dot_general(slopes, inputs, (((0,), (0,)), ((), ())), preferred_element_type=jnp.float32)
    return grad_up, grad_down


def reference(tokens, targets, token_counts, sample_counts, up_weight, down_weight, momentum_up, momentum_down):
    positions = jnp.arange(ROWS, dtype=jnp.int32)[:, None]

    def group_term(running, group_index):
        acc_up = jnp.zeros((FFW, D), jnp.float32)
        acc_down = jnp.zeros((FFW, D), jnp.float32)
        for slot_num in range(CL_GRP):
            client = (group_index * CL_GRP + slot_num).astype(jnp.int32)
            inputs = lax.dynamic_index_in_dim(tokens, client, 0, keepdims=False)
            target = lax.dynamic_index_in_dim(targets, client, 0, keepdims=False)
            valid_rows = lax.dynamic_index_in_dim(token_counts, client, 0, keepdims=False)
            row_mask = (positions < valid_rows).astype(jnp.float32)
            client_weight = lax.dynamic_index_in_dim(sample_counts, client, 0, keepdims=False).astype(jnp.float32)
            weight_up, weight_down = up_weight, down_weight
            for local_step in range(STEPS):
                grad_up, grad_down = client_grads(inputs, target, row_mask, weight_up, weight_down)
                acc_up = acc_up + client_weight * grad_up
                acc_down = acc_down + client_weight * grad_down
                if local_step + 1 < STEPS:
                    weight_up = (weight_up.astype(jnp.float32) - client_rate * grad_up).astype(jnp.bfloat16)
                    weight_down = (weight_down.astype(jnp.float32) - client_rate * grad_down).astype(jnp.bfloat16)
        group_up = lax.optimization_barrier(acc_up.astype(jnp.bfloat16)).astype(jnp.float32)
        group_down = lax.optimization_barrier(acc_down.astype(jnp.bfloat16)).astype(jnp.float32)
        return (running[0] + group_up, running[1] + group_down), jnp.zeros((), jnp.float32)

    start_sums = (jnp.zeros((FFW, D), jnp.float32), jnp.zeros((FFW, D), jnp.float32))
    (sum_up, sum_down), unused_out = lax.scan(group_term, start_sums, jnp.arange(N_GROUP, dtype=jnp.int32))
    weight_total = jnp.sum(sample_counts).astype(jnp.float32)
    new_momentum_up = momentum_decay * momentum_up + sum_up / weight_total
    new_momentum_down = momentum_decay * momentum_down + sum_down / weight_total
    return (new_momentum_up, new_momentum_down)
```

```python
import jax
import jax.numpy as jnp
from jax import lax
from jax.sharding import PartitionSpec as P

STEPS = 2
PAIR = 2

client_rate = 0.0003
momentum_decay = 0.9


def silu_slope(preact):
    logistic = jax.nn.sigmoid(preact)
    return logistic * (1.0 + preact * (1.0 - logistic))


def contract_cols(former, latter):
    return lax.dot_general(
        former, latter, (((1,), (1,)), ((), ())), preferred_element_type=jnp.float32
    )


def by_client(array, clients):
    return array.reshape(clients, array.shape[0] // clients, array.shape[1])


def gram(former, latter, clients):
    return jnp.einsum(
        "crk,cqk->crq",
        by_client(former, clients),
        by_client(latter, clients),
        preferred_element_type=jnp.float32,
    )


def correction(grams, factor, clients):
    wide = jnp.einsum(
        "crq,cqk->crk",
        client_rate * grams,
        by_client(factor, clients).astype(jnp.float32),
        precision=lax.Precision.HIGHEST,
        preferred_element_type=jnp.float32,
    )
    return wide.reshape(factor.shape)


def on_device(
    group_size,
    tokens,
    targets,
    token_counts,
    sample_counts,
    up_weight,
    down_weight,
    momentum_up,
    momentum_down,
):
    clients, row_count, own_width = tokens.shape
    hidden_count, width = up_weight.shape
    rows = clients * row_count
    block = width // group_size
    lines = group_size // PAIR
    group = lax.axis_index("group")
    low = lax.rem(group, PAIR)
    across = [(g, g ^ 1) for g in range(group_size)]

    def to_partner(array):
        return lax.ppermute(array, "group", across)

    def gather_cols(array):
        return lax.all_gather(array, "tensor", axis=1, tiled=True)

    inputs = gather_cols(tokens.reshape(rows, own_width))
    own_target = targets.reshape(rows, own_width).astype(jnp.float32)
    positions = jnp.arange(row_count, dtype=jnp.int32)[None, :]
    row_mask = (positions < token_counts[:, None]).astype(jnp.float32).reshape(rows, 1)
    client_weights = lax.dynamic_slice_in_dim(sample_counts, group * clients, clients).astype(
        jnp.float32
    )
    row_weight = jnp.repeat(client_weights, row_count)[:, None]

    def residual_of(partial_out):
        own_cols = lax.psum_scatter(
            partial_out.astype(jnp.bfloat16), "tensor", scatter_dimension=1, tiled=True
        ).astype(jnp.float32)
        return gather_cols((row_mask * (own_cols - own_target)).astype(jnp.bfloat16))

    def column_sets(factor):
        weighted = (row_weight * factor.astype(jnp.float32)).astype(jnp.bfloat16)
        sets = weighted.reshape(rows, lines, PAIR, block).transpose(2, 1, 0, 3)
        mine = lax.dynamic_index_in_dim(sets, low, 0, keepdims=False)
        other = lax.dynamic_index_in_dim(sets, 1 - low, 0, keepdims=False)
        return mine, to_partner(other)

    preact0 = contract_cols(inputs, up_weight)
    hidden0 = jax.nn.silu(preact0).astype(jnp.bfloat16)
    partial0 = jnp.dot(hidden0, down_weight, preferred_element_type=jnp.float32)
    hidden0_far = to_partner(hidden0)
    input_grams = gram(inputs, inputs, clients)
    input_cols = column_sets(inputs)
    residual0 = residual_of(partial0)
    slopes0 = (contract_cols(residual0, down_weight) * silu_slope(preact0)).astype(jnp.bfloat16)
    slopes0_far = to_partner(slopes0)

    preact1 = preact0 - correction(input_grams, slopes0, clients)
    hidden1 = jax.nn.silu(preact1).astype(jnp.bfloat16)
    partial1 = jnp.dot(
        hidden1, down_weight, preferred_element_type=jnp.float32
    ) - correction(gram(hidden1, hidden0, clients), residual0, clients)
    hidden1_far = to_partner(hidden1)
    residual0_cols = column_sets(residual0)
    residual1 = residual_of(partial1)
    residual1_cols = column_sets(residual1)
    back1 = contract_cols(residual1, down_weight) - correction(
        gram(residual1, residual0, clients), hidden0, clients
    )
    slopes1 = (back1 * silu_slope(preact1)).astype(jnp.bfloat16)
    slopes1_far = to_partner(slopes1)

    weight_total = jnp.sum(sample_counts).astype(jnp.float32)
    alike = [[line * PAIR + part for line in range(lines)] for part in range(PAIR)]

    def server_sum(left, right):
        pair_sum = jnp.einsum(
            "kf,nkc->nfc",
            jnp.concatenate(left, axis=0),
            jnp.concatenate(right, axis=1),
            preferred_element_type=jnp.float32,
        ).astype(jnp.bfloat16)
        return lax.psum_scatter(
            pair_sum.reshape(lines * hidden_count, block),
            "group",
            scatter_dimension=0,
            axis_index_groups=alike,
            tiled=True,
        ).astype(jnp.float32)

    sum_down = server_sum(
        (hidden0, hidden1, hidden0_far, hidden1_far),
        (residual0_cols[0], residual1_cols[0], residual0_cols[1], residual1_cols[1]),
    )
    sum_up = server_sum(
        (slopes0, slopes1, slopes0_far, slopes1_far),
        (input_cols[0], input_cols[0], input_cols[1], input_cols[1]),
    )
    new_momentum_up = momentum_decay * momentum_up + sum_up / weight_total
    new_momentum_down = momentum_decay * momentum_down + sum_down / weight_total
    return (new_momentum_up, new_momentum_down)


def solution(mesh):
    placed = (
        P("group", None, "tensor"),
        P("group", None, "tensor"),
        P("group"),
        P(),
        P("tensor", None),
        P("tensor", None),
        P("tensor", "group"),
        P("tensor", "group"),
    )
    group_size = mesh.shape["group"]

    def run(*args):
        return on_device(group_size, *args)

    return jax.shard_map(
        run,
        mesh=mesh,
        in_specs=placed,
        out_specs=(P("tensor", "group"), P("tensor", "group")),
        check_vma=False,
    )
```

```python
import jax
import jax.numpy as jnp
from jax import lax
from jax.sharding import PartitionSpec as P

STEPS = 2
PAIR = 2

client_rate = 0.0003
momentum_decay = 0.9


def silu_slope(preact):
    logistic = jax.nn.sigmoid(preact)
    return logistic * (1.0 + preact * (1.0 - logistic))


def contract_cols(former, latter):
    return lax.dot_general(
        former, latter, (((1,), (1,)), ((), ())), preferred_element_type=jnp.float32
    )


def by_client(array, clients):
    return array.reshape(clients, array.shape[0] // clients, array.shape[1])


def gram(former, latter, clients):
    return jnp.einsum(
        "crk,cqk->crq",
        by_client(former, clients),
        by_client(latter, clients),
        preferred_element_type=jnp.float32,
    )


def correction(grams, factor, clients):
    wide = jnp.einsum(
        "crq,cqk->crk",
        client_rate * grams,
        by_client(factor, clients).astype(jnp.float32),
        precision=lax.Precision.HIGHEST,
        preferred_element_type=jnp.float32,
    )
    return wide.reshape(factor.shape)


def on_device(
    group_size,
    tokens,
    targets,
    token_counts,
    sample_counts,
    up_weight,
    down_weight,
    momentum_up,
    momentum_down,
):
    clients, row_count, own_width = tokens.shape
    hidden_count, width = up_weight.shape
    rows = clients * row_count
    block = width // group_size
    lines = group_size // PAIR
    group = lax.axis_index("group")
    low = lax.rem(group, PAIR)
    across = [(g, g ^ 1) for g in range(group_size)]

    def to_partner(array):
        return lax.ppermute(array, "group", across)

    def gather_cols(array):
        return lax.all_gather(array, "tensor", axis=1, tiled=True)

    inputs = gather_cols(tokens.reshape(rows, own_width))
    own_target = targets.reshape(rows, own_width).astype(jnp.float32)
    positions = jnp.arange(row_count, dtype=jnp.int32)[None, :]
    row_mask = (positions < token_counts[:, None]).astype(jnp.float32).reshape(rows, 1)
    client_weights = lax.dynamic_slice_in_dim(sample_counts, group * clients, clients).astype(
        jnp.float32
    )
    row_weight = jnp.repeat(client_weights, row_count)[:, None]

    def residual_of(partial_out, early, late):
        own_cols = lax.psum_scatter(
            partial_out.astype(jnp.bfloat16), "tensor", scatter_dimension=1, tiled=True
        )
        own_cols, early = lax.optimization_barrier((own_cols, early))
        own_cols = own_cols.astype(jnp.float32)
        whole = gather_cols((row_mask * (own_cols - own_target)).astype(jnp.bfloat16))
        whole, late = lax.optimization_barrier((whole, late))
        return whole, early, late

    def column_sets(factor):
        weighted = (row_weight * factor.astype(jnp.float32)).astype(jnp.bfloat16)
        sets = weighted.reshape(rows, lines, PAIR, block).transpose(2, 1, 0, 3)
        mine = lax.dynamic_index_in_dim(sets, low, 0, keepdims=False)
        other = lax.dynamic_index_in_dim(sets, 1 - low, 0, keepdims=False)
        return mine, to_partner(other)

    preact0 = contract_cols(inputs, up_weight)
    hidden0 = jax.nn.silu(preact0).astype(jnp.bfloat16)
    partial0 = jnp.dot(hidden0, down_weight, preferred_element_type=jnp.float32)
    hidden0_far = to_partner(hidden0)
    input_grams = gram(inputs, inputs, clients)
    input_cols = column_sets(inputs)
    residual0, hidden0_far, input_cols = residual_of(partial0, hidden0_far, input_cols)
    slopes0 = (contract_cols(residual0, down_weight) * silu_slope(preact0)).astype(jnp.bfloat16)
    slopes0_far = to_partner(slopes0)

    preact1 = preact0 - correction(input_grams, slopes0, clients)
    hidden1 = jax.nn.silu(preact1).astype(jnp.bfloat16)
    partial1 = jnp.dot(
        hidden1, down_weight, preferred_element_type=jnp.float32
    ) - correction(gram(hidden1, hidden0, clients), residual0, clients)
    hidden1_far = to_partner(hidden1)
    residual0_cols = column_sets(residual0)
    residual1, (hidden1_far, slopes0_far), residual0_cols = residual_of(
        partial1, (hidden1_far, slopes0_far), residual0_cols
    )
    residual1_cols = column_sets(residual1)
    back1 = contract_cols(residual1, down_weight) - correction(
        gram(residual1, residual0, clients), hidden0, clients
    )
    slopes1 = (back1 * silu_slope(preact1)).astype(jnp.bfloat16)
    slopes1_far = to_partner(slopes1)

    weight_total = jnp.sum(sample_counts).astype(jnp.float32)
    alike = [[line * PAIR + part for line in range(lines)] for part in range(PAIR)]

    def server_sum(left, right):
        pair_sum = jnp.einsum(
            "nkc,kf->ncf",
            jnp.concatenate(right, axis=1),
            jnp.concatenate(left, axis=0),
            preferred_element_type=jnp.float32,
        ).astype(jnp.bfloat16)
        return lax.psum_scatter(
            pair_sum.reshape(lines * block, hidden_count),
            "group",
            scatter_dimension=0,
            axis_index_groups=alike,
            tiled=True,
        ).T.astype(jnp.float32)

    sum_down = server_sum(
        (hidden0, hidden1, hidden0_far, hidden1_far),
        (residual0_cols[0], residual1_cols[0], residual0_cols[1], residual1_cols[1]),
    )
    sum_up = server_sum(
        (slopes0, slopes1, slopes0_far, slopes1_far),
        (input_cols[0], input_cols[0], input_cols[1], input_cols[1]),
    )
    new_momentum_up = momentum_decay * momentum_up + sum_up / weight_total
    new_momentum_down = momentum_decay * momentum_down + sum_down / weight_total
    return (new_momentum_up, new_momentum_down)


def solution(mesh):
    placed = (
        P("group", None, "tensor"),
        P("group", None, "tensor"),
        P("group"),
        P(),
        P("tensor", None),
        P("tensor", None),
        P("tensor", "group"),
        P("tensor", "group"),
    )
    group_size = mesh.shape["group"]

    def run(*args):
        return on_device(group_size, *args)

    return jax.shard_map(
        run,
        mesh=mesh,
        in_specs=placed,
        out_specs=(P("tensor", "group"), P("tensor", "group")),
        check_vma=False,
    )
```

```python
import jax
import jax.numpy as jnp
from jax import lax
from jax.sharding import PartitionSpec as P

STEPS = 2
PAIR = 2

client_rate = 0.0003
momentum_decay = 0.9


def silu_slope(preact):
    logistic = jax.nn.sigmoid(preact)
    return logistic * (1.0 + preact * (1.0 - logistic))


def contract_cols(former, latter):
    return lax.dot_general(
        former, latter, (((1,), (1,)), ((), ())), preferred_element_type=jnp.float32
    )


def by_client(array, clients):
    return array.reshape(clients, array.shape[0] // clients, array.shape[1])


def gram(former, latter, clients):
    return jnp.einsum(
        "crk,cqk->crq",
        by_client(former, clients),
        by_client(latter, clients),
        preferred_element_type=jnp.float32,
    )


def correction(grams, factor, clients):
    wide = jnp.einsum(
        "crq,cqk->crk",
        client_rate * grams,
        by_client(factor, clients).astype(jnp.float32),
        precision=lax.Precision.HIGHEST,
        preferred_element_type=jnp.float32,
    )
    return wide.reshape(factor.shape)


def on_device(
    group_size,
    tokens,
    targets,
    token_counts,
    sample_counts,
    up_weight,
    down_weight,
    momentum_up,
    momentum_down,
):
    clients, row_count, own_width = tokens.shape
    hidden_count, width = up_weight.shape
    rows = clients * row_count
    block = width // group_size
    lines = group_size // PAIR
    group = lax.axis_index("group")
    low = lax.rem(group, PAIR)
    across = [(g, g ^ 1) for g in range(group_size)]

    def to_partner(array):
        return lax.ppermute(array, "group", across)

    def gather_cols(array):
        return lax.all_gather(array, "tensor", axis=1, tiled=True)

    inputs = gather_cols(tokens.reshape(rows, own_width))
    own_target = targets.reshape(rows, own_width).astype(jnp.float32)
    positions = jnp.arange(row_count, dtype=jnp.int32)[None, :]
    row_mask = (positions < token_counts[:, None]).astype(jnp.float32).reshape(rows, 1)
    client_weights = lax.dynamic_slice_in_dim(sample_counts, group * clients, clients).astype(
        jnp.float32
    )
    row_weight = jnp.repeat(client_weights, row_count)[:, None]

    def residual_of(partial_out, early, late):
        own_cols = lax.psum_scatter(
            partial_out.astype(jnp.bfloat16), "tensor", scatter_dimension=1, tiled=True
        )
        own_cols, early = lax.optimization_barrier((own_cols, early))
        own_cols = own_cols.astype(jnp.float32)
        whole = gather_cols((row_mask * (own_cols - own_target)).astype(jnp.bfloat16))
        whole, late = lax.optimization_barrier((whole, late))
        return whole, early, late

    def column_sets(factor):
        weighted = (row_weight * factor.astype(jnp.float32)).astype(jnp.bfloat16)
        sets = weighted.reshape(rows, lines, PAIR, block).transpose(2, 1, 0, 3)
        mine = lax.dynamic_index_in_dim(sets, low, 0, keepdims=False)
        other = lax.dynamic_index_in_dim(sets, 1 - low, 0, keepdims=False)
        return mine, to_partner(other)

    alike = [[line * PAIR + part for line in range(lines)] for part in range(PAIR)]
    line = group // PAIR

    def gather_lines(factor):
        return lax.all_gather(factor, "group", axis=0, axis_index_groups=alike, tiled=True)

    def line_columns(factor):
        weighted = (row_weight * factor.astype(jnp.float32)).astype(jnp.bfloat16)
        sets = weighted.reshape(rows, lines, PAIR * block).transpose(1, 0, 2)
        found = [lax.dynamic_index_in_dim(sets, line, 0, keepdims=False)]
        for shift in range(1, lines):
            moves = [
                (at * PAIR + part, (at + shift) % lines * PAIR + part)
                for at in range(lines)
                for part in range(PAIR)
            ]
            leaving = lax.dynamic_index_in_dim(sets, (line + shift) % lines, 0, keepdims=False)
            found.append(lax.ppermute(leaving, "group", moves))
        return found

    def in_line_order(found):
        order = (line - jnp.arange(lines)) % lines
        return jnp.stack(found)[order].reshape(lines * rows, PAIR * block)

    preact0 = contract_cols(inputs, up_weight)
    hidden0 = jax.nn.silu(preact0).astype(jnp.bfloat16)
    partial0 = jnp.dot(hidden0, down_weight, preferred_element_type=jnp.float32)
    input_grams = gram(inputs, inputs, clients)
    input_cols = column_sets(inputs)
    residual0, _, input_cols = residual_of(partial0, (), input_cols)
    residual0, hidden0 = lax.optimization_barrier((residual0, hidden0))
    hidden0_all = gather_lines(hidden0)
    slopes0 = (contract_cols(residual0, down_weight) * silu_slope(preact0)).astype(jnp.bfloat16)
    slopes0_far = to_partner(slopes0)

    preact1 = preact0 - correction(input_grams, slopes0, clients)
    hidden1 = jax.nn.silu(preact1).astype(jnp.bfloat16)
    partial1 = jnp.dot(
        hidden1, down_weight, preferred_element_type=jnp.float32
    ) - correction(gram(hidden1, hidden0, clients), residual0, clients)
    residual0_cols = line_columns(residual0)
    residual1, hidden0_all, (slopes0_far, residual0_cols) = residual_of(
        partial1, hidden0_all, (slopes0_far, residual0_cols)
    )
    residual1, hidden1 = lax.optimization_barrier((residual1, hidden1))
    hidden1_all = gather_lines(hidden1)
    residual1_cols = line_columns(residual1)
    back1 = contract_cols(residual1, down_weight) - correction(
        gram(residual1, residual0, clients), hidden0, clients
    )
    slopes1 = (back1 * silu_slope(preact1)).astype(jnp.bfloat16)
    slopes1_far = to_partner(slopes1)
    slopes1_far, hidden1_all = lax.optimization_barrier((slopes1_far, hidden1_all))

    weight_total = jnp.sum(sample_counts).astype(jnp.float32)

    pair_sum = jnp.einsum(
        "nkc,kf->ncf",
        jnp.concatenate((input_cols[0], input_cols[0], input_cols[1], input_cols[1]), axis=1),
        jnp.concatenate((slopes0, slopes1, slopes0_far, slopes1_far), axis=0),
        preferred_element_type=jnp.float32,
    ).astype(jnp.bfloat16)
    sum_up = lax.psum_scatter(
        pair_sum.reshape(lines * block, hidden_count),
        "group",
        scatter_dimension=0,
        axis_index_groups=alike,
        tiled=True,
    ).T.astype(jnp.float32)

    line_hidden = jnp.concatenate((hidden0_all, hidden1_all), axis=0)
    line_cols = jnp.concatenate((in_line_order(residual0_cols), in_line_order(residual1_cols)))
    line_sum = jnp.einsum(
        "kc,kf->cf", line_cols, line_hidden, preferred_element_type=jnp.float32
    ).astype(jnp.bfloat16).reshape(PAIR, block, hidden_count)
    kept = lax.dynamic_index_in_dim(line_sum, low, 0, keepdims=False)
    came = to_partner(lax.dynamic_index_in_dim(line_sum, 1 - low, 0, keepdims=False))
    sum_down = (kept.astype(jnp.float32) + came.astype(jnp.float32)).T
    new_momentum_up = momentum_decay * momentum_up + sum_up / weight_total
    new_momentum_down = momentum_decay * momentum_down + sum_down / weight_total
    return (new_momentum_up, new_momentum_down)


def solution(mesh):
    placed = (
        P("group", None, "tensor"),
        P("group", None, "tensor"),
        P("group"),
        P(),
        P("tensor", None),
        P("tensor", None),
        P("tensor", "group"),
        P("tensor", "group"),
    )
    group_size = mesh.shape["group"]

    def run(*args):
        return on_device(group_size, *args)

    return jax.shard_map(
        run,
        mesh=mesh,
        in_specs=placed,
        out_specs=(P("tensor", "group"), P("tensor", "group")),
        check_vma=False,
    )
```
